32 devices in a mesh: row: 16 (over z, y, core), col: 2 (over x).
Axes of the slice: x: 2, y: 2, z: 4, core: 2. Of those that a mesh axis runs over, the one named last changes fastest.
Arguments:
- features: bfloat16 [16384, 128], P(('col', 'row')), may hold values from -6 to 6
- weight: bfloat16 [128, 172], replicated, may hold values from -0.5 to 0.5
- labels: int32 [16384], P(('row', 'col')), may hold values from -43 to 171
- tile_rows: int32 [16, 2, 256], P('row', 'col'), may hold values from 0 to 7, as said below
- tile_cols: int32 [16, 2, 256], P('row', 'col'), may hold values from 0 to 63
- tile_count: int32 [16, 2], P('row', 'col'), may hold values from 1 to 256, as said below
- tile_vals: bfloat16 [16, 2, 256, 128, 128], P('row', 'col'), may hold values from -0.07470703 to 0.07470703
Outputs:
- logits: float32 [16384, 172], P(('row', 'col'))
- weight_grad: float32 [128, 172], replicated
The draws below stay inside these ranges and needn't reach their ends.
Inputs may be any that keep to these rules, and one draw needn't show every extreme that they name: `tile_rows`: within one device the used slots name distinct tiles; unused slots are ignored. `tile_count`: counts differ between devices; in every draw some device uses all 256 slots.
All inputs are finite; a program needn't handle non-finite values.
Results may differ from the reference program's by a relative error of at most 0.0029.
Values may be sent and summed in bfloat16 or wider, within the bound.
A program may use at most 128 MiB of HBM per device.

```python
import jax
import jax.numpy as jnp
from jax import lax

FEAT = 128
CLASSES = 172
TILE = 128
TMAX = 256
ROW_TILES = 8
COL_TILES = 64
NODES = 16384
N_ROW = 16
N_COL = 2


def tile_places(key):
    keys = jax.random.split(key, N_ROW * N_COL)
    picked = jax.vmap(lambda k: jax.random.permutation(k, ROW_TILES * COL_TILES)[:TMAX])(keys)
    return picked.reshape(N_ROW, N_COL, TMAX).astype(jnp.int32)


def draw_tile_rows(key, part):
    return tile_places(key) // COL_TILES


def draw_tile_cols(key, part):
    return tile_places(key) % COL_TILES


def draw_tile_count(key, part):
    key = jax.random.fold_in(key, 7)
    key_a, key_b = jax.random.split(key)
    counts = jax.random.randint(key_a, (N_ROW * N_COL,), max(1, TMAX // 8), TMAX // 2 + 1)
    busiest = jax.random.randint(key_b, (), 0, N_ROW * N_COL)
    counts = jnp.where(jnp.arange(N_ROW * N_COL) == busiest, TMAX, counts)
    return counts.reshape(N_ROW, N_COL).astype(jnp.int32)


def plant(entries, rng, smallest, top_value):
    dims = entries.shape
    spot = [jax.random.randint(jax.random.fold_in(rng, axis), (), 0, dims[axis]) for axis in range(len(dims))]
    entries = entries.at[tuple(spot)].set(smallest)
    longest = dims.index(max(dims))
    spot[longest] = (spot[longest] + 1) % dims[longest]
    return entries.at[tuple(spot)].set(top_value)


def block_scale(rng, dims, pieces, low, largest):
    level, own = 1.0, jax.random.fold_in(rng, 6)
    for dim, blocks in pieces:
        steps = jnp.exp(jax.random.uniform(jax.random.fold_in(own, dim), (blocks,), jnp.float32, low / len(pieces), largest / len(pieces)))
        level = level * jnp.repeat(steps, dims[dim] // blocks).reshape([-1 if axis == dim else 1 for axis in range(len(dims))])
    return level


def gaussian(rng, shape, spread, most, cuts=(), held_as=jnp.bfloat16):
    entries = spread * jax.random.normal(rng, shape, jnp.float32)
    if cuts:
        entries = entries * block_scale(rng, shape, cuts, -0.22, 0.18)
    return jnp.clip(entries, -most, most).astype(held_as)


def setup_inputs(seed: int = 0) -> dict:
    streams_of = jax.random.split(jax.random.key(seed), 8)
    features = gaussian(streams_of[0], (NODES, FEAT), 1.0, 6.0, ((0, 32),))
    weight = gaussian(streams_of[1], (FEAT, CLASSES), FEAT ** -0.5, 0.5)
    labels = plant(jax.random.randint(streams_of[2], (NODES,), 0 - CLASSES // 4, CLASSES), jax.random.fold_in(streams_of[2], 1), 0 - CLASSES // 4, CLASSES - 1).astype(jnp.int32)
    tile_rows = draw_tile_rows(jax.random.fold_in(streams_of[7], 71), 0)
    tile_cols = draw_tile_cols(jax.random.fold_in(streams_of[7], 71), 0)
    tile_count = draw_tile_count(jax.random.fold_in(streams_of[7], 71), 0)
    tile_vals = gaussian(streams_of[6], (N_ROW, N_COL, TMAX, TILE, TILE), 0.0125, 0.07470703, ((0, 16), (1, 2)))
    return {"features": features, "weight": weight, "labels": labels, "tile_rows": tile_rows, "tile_cols": tile_cols, "tile_count": tile_count, "tile_vals": tile_vals}


def aggregate(table, gather_idx, scatter_idx, vals, count, out_tiles, transpose):
    blk = min(32, vals.shape[0])
    classes = table.shape[-1]
    nblk = (count + blk - 1) // blk

    def step(b, acc):
        start = (b * blk).astype(jnp.int32)
        piece = lax.dynamic_slice_in_dim(vals, start, blk, 0).astype(jnp.float32)
        gidx = lax.dynamic_slice_in_dim(gather_idx, start, blk, 0)
        sidx = lax.dynamic_slice_in_dim(scatter_idx, start, blk, 0)
        sel = table[gidx].astype(jnp.float32)
        if transpose:
            prod = jnp.einsum('tji,tjc->tic', piece, sel)
        else:
            prod = jnp.einsum('tij,tjc->tic', piece, sel)
        valid = (start + jnp.arange(blk, dtype=jnp.int32) < count).astype(jnp.float32)
        return acc.at[sidx].add(prod * valid[:, None, None])
    init = jnp.zeros((out_tiles, table.shape[1], classes), jnp.float32)
    return lax.fori_loop(0, nblk, step, init)

def reference(features, weight, labels, tile_rows, tile_cols, tile_count, tile_vals):
    classes = weight.shape[1]
    row_len = ROW_TILES * TILE
    col_len = COL_TILES * TILE
    projected = jnp.dot(features, weight, preferred_element_type=jnp.float32).astype(jnp.bfloat16)

    def forward(idx, acc):
        r = idx // N_COL
        c = idx % N_COL
        block = lax.dynamic_slice_in_dim(projected, (c * col_len).astype(jnp.int32), col_len, 0)
        table = block.reshape(COL_TILES, TILE, classes)
        part = aggregate(table, tile_cols[r, c], tile_rows[r, c], tile_vals[r, c], tile_count[r, c], ROW_TILES, False)
        start = (r * row_len).astype(jnp.int32)
        old = lax.dynamic_slice_in_dim(acc, start, row_len, 0)
        return lax.dynamic_update_slice_in_dim(acc, old + part.reshape(row_len, classes), start, 0)
    logits = lax.fori_loop(0, N_ROW * N_COL, forward, jnp.zeros((NODES, classes), jnp.float32))
    onehot = (labels[:, None] == jnp.arange(classes, dtype=jnp.int32)[None, :]).astype(jnp.float32)
    residual_grad = jnp.where(labels[:, None] >= 0, logits - onehot, 0.0).astype(jnp.bfloat16)

    def backward(idx, acc):
        r = idx // N_COL
        c = idx % N_COL
        block = lax.dynamic_slice_in_dim(residual_grad, (r * row_len).astype(jnp.int32), row_len, 0)
        table = block.reshape(ROW_TILES, TILE, classes)
        part = aggregate(table, tile_rows[r, c], tile_cols[r, c], tile_vals[r, c], tile_count[r, c], COL_TILES, True)
        start = (c * col_len).astype(jnp.int32)
        old = lax.dynamic_slice_in_dim(acc, start, col_len, 0)
        return lax.dynamic_update_slice_in_dim(acc, old + part.reshape(col_len, classes), start, 0)
    projected_grad = lax.fori_loop(0, N_ROW * N_COL, backward, jnp.zeros((NODES, classes), jnp.float32))
    weight_grad = jnp.dot(features.astype(jnp.float32).T, projected_grad, precision=lax.Precision.HIGHEST)
    weight_grad = weight_grad / jnp.sqrt(jnp.float32(NODES))
    return (logits, weight_grad)
```

```python
import functools
import math

import jax
import jax.numpy as jnp
from jax import lax
from jax.experimental import pallas as pl
from jax.experimental.pallas import tpu as pltpu
from jax.sharding import PartitionSpec as P

F32, BF16 = jnp.float32, jnp.bfloat16
MESH = pl.DeviceIdType.MESH


def factors(n_row):
    cores = 2 if n_row % 2 == 0 else 1
    chips = n_row // cores
    la = 4 if chips % 4 == 0 else chips
    return la, chips // la, cores


def nearest(pos, size, n):
    out = 0
    for p in range(size):
        order = sorted(range(size), key=lambda s: (abs(s - p), s))
        out = out + jnp.where(pos == p, order[n], 0)
    return out


def split(x):
    hi = x.astype(BF16)
    return hi, (x - hi.astype(F32)).astype(BF16)


def dot(a, b):
    return jnp.dot(a, b, preferred_element_type=F32)


def kernel(dims, feat, weight, labels, tab, vals, logits, wgrad,
           x, tiles, acc1, acc2, out2, in1, in2,
           ssem, rsem, vsem, s1, r1, s2, r2):
    n_row, n_col, la, lb, cores, scale = dims
    slots, tile = vals.shape[0], vals.shape[1]
    rt, bt = acc1.shape[0], feat.shape[0] // tile
    ct = n_row * bt
    row, col = lax.axis_index("row"), lax.axis_index("col")
    core = row % cores
    q = (row // cores) % lb
    p = row // (cores * lb)

    def place(s, t, c):
        return (s * lb + t) * cores + c

    def when(cond, fn):
        if cond is True:
            fn()
        else:
            pl.when(cond)(fn)

    fetch = pltpu.make_async_copy(vals, tiles.at[pl.ds(0, slots)], vsem)
    fetch.start()

    barrier = pltpu.get_barrier_semaphore()
    peers = [(p + 1 < la, place(p + 1, q, core)), (p > 0, place(p - 1, q, core)),
             (q + 1 < lb, place(p, q + 1, core)), (q > 0, place(p, q - 1, core))]
    if cores == 2:
        peers.append((True, place(p, q, 1 - core)))
    for cond, where in peers:
        when(cond, functools.partial(pl.semaphore_signal, barrier, inc=1, device_id={"row": where}, device_id_type=MESH))
    for k in range(1, n_col):
        pl.semaphore_signal(barrier, inc=1, device_id={"col": (col + k) % n_col}, device_id_type=MESH)
    x[row] = feat[...]
    tiles[slots] = jnp.zeros((tile, tile), BF16)
    count = n_col - 1 + (cores - 1)
    for cond, _ in peers[:4]:
        count = count + jnp.where(cond, 1, 0)
    pl.semaphore_wait(barrier, count)

    started = []

    def send(cond, step, way, block, where):
        copy = pltpu.make_async_remote_copy(
            src_ref=x.at[block], dst_ref=x.at[block], send_sem=ssem.at[step, way], recv_sem=rsem.at[block],
            device_id={"row": where}, device_id_type=MESH)
        when(cond, copy.start)
        started.append((cond, copy))

    def arrive(block):
        pltpu.make_async_remote_copy(
            src_ref=x.at[block], dst_ref=x.at[block], send_sem=ssem.at[0, 0], recv_sem=rsem.at[block],
            device_id={"row": (row + 1) % n_row}, device_id_type=MESH).wait_recv()

    def forward(na, nb, s, t):
        block, step = place(s, t, core), na * lb + nb
        if nb == 0:
            up = p + 1 < la if na == 0 else jnp.logical_and(s < p, p + 1 < la)
            down = p > 0 if na == 0 else jnp.logical_and(s > p, p > 0)
            send(up, step, 0, block, place(p + 1, q, core))
            send(down, step, 1, block, place(p - 1, q, core))
            send(q + 1 < lb, step, 2, block, place(p, q + 1, core))
            send(q > 0, step, 3, block, place(p, q - 1, core))
        elif lb > 2:
            send(jnp.logical_and(t < q, q + 1 < lb), step, 2, block, place(p, q + 1, core))
            send(jnp.logical_and(t > q, q > 0), step, 3, block, place(p, q - 1, core))
        if cores == 2:
            send(True, step, 4, block, place(p, q, 1 - core))

    def multiply(block, acc, lo, hi, first=False):
        def body(n, carry):
            i = ((col + 1) * bt + n) % rt
            at = i * ct + block * bt
            lhs = jnp.concatenate([tiles[tab[at + m]] for m in range(bt)], axis=1)
            y = dot(lhs, x[block])
            acc[i] = y if first else acc[i] + y
            return carry
        lax.fori_loop(lo, hi, body, 0, unroll=2)

    groups = [[(step - nb, nb) for nb in range(lb) if 0 <= step - nb < la] for step in range(la + lb - 1)]
    early = max(1, len(groups) - 2)
    exchange1, exchange2 = [], []
    tail = []
    for g, group in enumerate(groups):
        places = [(na, nb, nearest(p, la, na), nearest(q, lb, nb)) for na, nb in group]
        for na, nb, s, t in places:
            if g > 0:
                arrive(place(s, t, core))
            forward(na, nb, s, t)
        if g == 0:
            fetch.wait()
        todo = [(place(s, t, core), False) for _, _, s, t in places]
        if cores == 2:
            todo += [(place(s, t, 1 - core), True) for _, _, s, t in places]
        acc = acc1 if g < early else acc2
        last = g == len(groups) - 1
        for n, (block, remote) in enumerate(todo):
            if remote:
                arrive(block)
            first = g in (0, early) and n == 0
            if last:
                multiply(block, acc, 0, rt - bt, first)
                tail.append((block, first))
            else:
                multiply(block, acc, 0, rt, first)
        if g == early - 1:
            for k in range(1, n_col):
                to = (col + k) % n_col
                copy = pltpu.make_async_remote_copy(
                    src_ref=acc1.at[pl.ds(to * bt, bt)], dst_ref=in1.at[k - 1], send_sem=s1.at[k - 1],
                    recv_sem=r1.at[k - 1], device_id={"col": to}, device_id_type=MESH)
                copy.start()
                exchange1.append(copy)
    for k in range(1, n_col):
        to = (col + k) % n_col
        out2[k - 1] = acc2[pl.ds(to * bt, bt)].astype(BF16)
        copy = pltpu.make_async_remote_copy(
            src_ref=out2.at[k - 1], dst_ref=in2.at[k - 1], send_sem=s2.at[k - 1],
            recv_sem=r2.at[k - 1], device_id={"col": to}, device_id_type=MESH)
        copy.start()
        exchange2.append(copy)
    for block, first in tail:
        multiply(block, acc2, rt - bt, rt, first)
    for cond, copy in started:
        when(cond, copy.wait_send)

    y = acc1[pl.ds(col * bt, bt)] + acc2[pl.ds(col * bt, bt)]
    for n, copy in enumerate(exchange1):
        copy.wait()
        y = y + in1[n]
    for n, copy in enumerate(exchange2):
        copy.wait()
        y = y + in2[n].astype(F32)
    y = y.reshape(bt * tile, tile)

    w = weight[...]
    hi, lo = split(y)
    logits[...] = dot(hi, w) + dot(lo, w)
    lab = labels[...]
    padded = -(-w.shape[1] // tile) * tile
    onehot = (lax.broadcasted_iota(jnp.int32, (padded, bt * tile), 0) == lab).astype(F32).astype(BF16)
    picked = dot(onehot, hi) + dot(onehot, lo)
    hi_t, lo_t = split(y.T * jnp.where(lab >= 0, 1.0, 0.0).astype(F32))
    gram_hi, gram_lo = split(dot(hi_t, hi) + dot(hi_t, lo) + dot(lo_t, hi))
    total = dot(gram_hi, w) + dot(gram_lo, w) - picked.T[:, : w.shape[1]]
    wgrad[...] = total * scale


def local(n_row, n_col, features, weight, labels, tile_rows, tile_cols, tile_count, tile_vals):
    la, lb, cores = factors(n_row)
    classes, tile, slots = weight.shape[1], tile_vals.shape[-1], tile_vals.shape[2]
    own, feat = features.shape
    bt = own // tile
    rt, ct = n_col * bt, n_row * bt
    nodes = own * n_row * n_col
    key = jnp.where(jnp.arange(slots, dtype=jnp.int32) < tile_count.reshape(()),
                    tile_rows.reshape(slots) * ct + tile_cols.reshape(slots), -1)
    match = key[:, None] == jnp.arange(rt * ct, dtype=jnp.int32)[None, :]
    table = slots + jnp.sum(jnp.where(match, jnp.arange(slots, dtype=jnp.int32)[:, None] - slots, 0), axis=0)
    dims = (n_row, n_col, la, lb, cores, 1.0 / math.sqrt(nodes))
    vmem = pl.BlockSpec(memory_space=pltpu.VMEM)
    dma = pltpu.SemaphoreType.DMA
    peers = max(1, n_col - 1)
    logits, wgrad = pl.pallas_call(
        functools.partial(kernel, dims),
        out_shape=(jax.ShapeDtypeStruct((own, classes), F32), jax.ShapeDtypeStruct((feat, classes), F32)),
        in_specs=[vmem, vmem, vmem, pl.BlockSpec(memory_space=pltpu.SMEM), pl.BlockSpec(memory_space=pl.ANY)],
        out_specs=(vmem, vmem),
        scratch_shapes=[
            pltpu.VMEM((n_row, own, feat), BF16),
            pltpu.VMEM((slots + 1, tile, tile), BF16),
            pltpu.VMEM((rt, tile, feat), F32),
            pltpu.VMEM((rt, tile, feat), F32),
            pltpu.VMEM((peers, bt, tile, feat), BF16),
            pltpu.VMEM((peers, bt, tile, feat), F32),
            pltpu.VMEM((peers, bt, tile, feat), BF16),
            dma((la * lb, 5)), dma((n_row,)), dma(()),
            dma((peers,)), dma((peers,)), dma((peers,)), dma((peers,)),
        ],
        compiler_params=pltpu.CompilerParams(collective_id=0, has_side_effects=True, vmem_limit_bytes=48 * 2**20),
        cost_estimate=pl.CostEstimate(flops=2 * rt * ct * tile * tile * feat, bytes_accessed=slots * tile * tile * 2, transcendentals=0),
        name="aggregate",
    )(features, weight, labels.reshape(1, own), table, tile_vals.reshape(slots, tile, tile))
    return logits, lax.psum(wgrad, ("row", "col"))


def solution(mesh):
    placed = (
        P(("col", "row"), None),
        P(),
        P(("row", "col")),
        P("row", "col", None),
        P("row", "col", None),
        P("row", "col"),
        P("row", "col", None, None, None),
    )
    body = functools.partial(local, mesh.shape["row"], mesh.shape["col"])
    return jax.shard_map(
        body, mesh=mesh, in_specs=placed, out_specs=(P(("row", "col"), None), P()), check_vma=False
    )
```

```python
import functools
import math

import jax
import jax.numpy as jnp
from jax import lax
from jax.experimental import pallas as pl
from jax.experimental.pallas import tpu as pltpu
from jax.sharding import PartitionSpec as P

F32, BF16 = jnp.float32, jnp.bfloat16
MESH = pl.DeviceIdType.MESH


def factors(n_row):
    cores = 2 if n_row % 2 == 0 else 1
    chips = n_row // cores
    la = 4 if chips % 4 == 0 else chips
    return la, chips // la, cores


def nearest(pos, size, n):
    out = 0
    for p in range(size):
        order = sorted(range(size), key=lambda s: (abs(s - p), s))
        out = out + jnp.where(pos == p, order[n], 0)
    return out


def split(x):
    hi = x.astype(BF16)
    return hi, (x - hi.astype(F32)).astype(BF16)


def dot(a, b):
    return jnp.dot(a, b, preferred_element_type=F32)


def kernel(dims, feat, weight, labels, tab, vals, logits, wgrad,
           x, tiles, acc1, acc2, out2, in1, in2, part, terms, summed,
           ssem, rsem, vsem, fsem, s1, r1, s2, r2, s3, r3, s4, r4):
    n_row, n_col, la, lb, cores, scale = dims
    slots, tile = vals.shape[0], vals.shape[1]
    bt = feat.shape[0] // tile
    ct = n_row * bt
    row, col = lax.axis_index("row"), lax.axis_index("col")
    core = row % cores
    q = (row // cores) % lb
    p = row // (cores * lb)

    def place(s, t, c):
        return (s * lb + t) * cores + c

    def when(cond, fn):
        if cond is True:
            fn()
        else:
            pl.when(cond)(fn)

    devices = n_row * n_col
    me = row * n_col + col

    def device(index):
        return (index // n_col, index % n_col)

    own = pltpu.make_async_copy(feat, x.at[row], fsem)
    own.start()
    pieces = vsem.shape[0]
    fetches = [pltpu.make_async_copy(vals.at[pl.ds(n * (slots // pieces), slots // pieces)],
                                     tiles.at[pl.ds(n * (slots // pieces), slots // pieces)], vsem.at[n])
               for n in range(pieces)]
    for copy in fetches:
        copy.start()

    barrier = pltpu.get_barrier_semaphore()

    def greet(k, carry):
        pl.semaphore_signal(barrier, inc=1, device_id=device((me + k) % devices), device_id_type=MESH)
        return carry
    lax.fori_loop(1, devices, greet, 0)
    tiles[slots] = jnp.zeros((tile, tile), BF16)
    own.wait()
    pl.semaphore_wait(barrier, devices - 1)

    started = []

    def send(cond, step, way, block, where):
        copy = pltpu.make_async_remote_copy(
            src_ref=x.at[block], dst_ref=x.at[block], send_sem=ssem.at[step, way], recv_sem=rsem.at[block],
            device_id={"row": where}, device_id_type=MESH)
        when(cond, copy.start)
        started.append((cond, copy))

    def arrive(block):
        pltpu.make_async_remote_copy(
            src_ref=x.at[block], dst_ref=x.at[block], send_sem=ssem.at[0, 0], recv_sem=rsem.at[block],
            device_id={"row": (row + 1) % n_row}, device_id_type=MESH).wait_recv()

    def forward(na, nb, s, t):
        block, step = place(s, t, core), na * lb + nb
        if nb == 0:
            up = p + 1 < la if na == 0 else jnp.logical_and(s < p, p + 1 < la)
            down = p > 0 if na == 0 else jnp.logical_and(s > p, p > 0)
            send(up, step, 0, block, place(p + 1, q, core))
            send(down, step, 1, block, place(p - 1, q, core))
            send(q + 1 < lb, step, 2, block, place(p, q + 1, core))
            send(q > 0, step, 3, block, place(p, q - 1, core))
        elif lb > 2:
            send(jnp.logical_and(t < q, q + 1 < lb), step, 2, block, place(p, q + 1, core))
            send(jnp.logical_and(t > q, q > 0), step, 3, block, place(p, q - 1, core))
        if cores == 2:
            send(True, step, 4, block, place(p, q, 1 - core))

    def multiply(block, acc, lo, hi, first=False):
        def body(n, carry):
            chunk = (col + n) % n_col
            lines = []
            for i in range(bt):
                at = (chunk * bt + i) * ct + block * bt
                lines.append(jnp.concatenate([tiles[tab[at + m]] for m in range(bt)], axis=1))
            y = dot(jnp.concatenate(lines, axis=0), x[block]).reshape(bt, tile, acc1.shape[2])
            rows = pl.ds(chunk * bt, bt)
            acc[rows] = y if first else acc[rows] + y
            return carry
        lax.fori_loop(lo, hi, body, 0, unroll=2 if (hi - lo) % 2 == 0 else 1)

    groups = [[(step - nb, nb) for nb in range(lb) if 0 <= step - nb < la] for step in range(la + lb - 1)]
    early = max(1, len(groups) - 2)
    exchange1, exchange2 = [], []
    tail = []
    for g, group in enumerate(groups):
        places = [(na, nb, nearest(p, la, na), nearest(q, lb, nb)) for na, nb in group]
        for na, nb, s, t in places:
            if g > 0:
                arrive(place(s, t, core))
            forward(na, nb, s, t)
        if g == 0:
            for copy in fetches:
                copy.wait()
        todo = [(place(s, t, core), False) for _, _, s, t in places]
        if cores == 2:
            todo += [(place(s, t, 1 - core), True) for _, _, s, t in places]
        acc = acc1 if g < early else acc2
        last = g == len(groups) - 1
        for n, (block, remote) in enumerate(todo):
            if remote:
                arrive(block)
            first = g in (0, early) and n == 0
            if last:
                multiply(block, acc, 1, n_col, first)
                tail.append((block, first))
            else:
                multiply(block, acc, 1, n_col + 1, first)
        if g == early - 1:
            for k in range(1, n_col):
                to = (col + k) % n_col
                copy = pltpu.make_async_remote_copy(
                    src_ref=acc1.at[pl.ds(to * bt, bt)], dst_ref=in1.at[k - 1], send_sem=s1.at[k - 1],
                    recv_sem=r1.at[k - 1], device_id={"col": to}, device_id_type=MESH)
                copy.start()
                exchange1.append(copy)
    for k in range(1, n_col):
        to = (col + k) % n_col
        out2[k - 1] = acc2[pl.ds(to * bt, bt)].astype(BF16)
        copy = pltpu.make_async_remote_copy(
            src_ref=out2.at[k - 1], dst_ref=in2.at[k - 1], send_sem=s2.at[k - 1],
            recv_sem=r2.at[k - 1], device_id={"col": to}, device_id_type=MESH)
        copy.start()
        exchange2.append(copy)
    for block, first in tail:
        multiply(block, acc2, n_col, n_col + 1, first)
    for cond, copy in started:
        when(cond, copy.wait_send)

    y = acc1[pl.ds(col * bt, bt)] + acc2[pl.ds(col * bt, bt)]
    for n, copy in enumerate(exchange1):
        copy.wait()
        y = y + in1[n]
    for n, copy in enumerate(exchange2):
        copy.wait()
        y = y + in2[n].astype(F32)
    y = y.reshape(bt * tile, tile)

    w = weight[...]
    classes = w.shape[0]
    hi, lo = split(y)
    y_t = y.T
    lab = labels[...]
    onehot = (lax.broadcasted_iota(jnp.int32, (classes, bt * tile), 0) == lab).astype(F32).astype(BF16)
    hi_v, lo_v = split(y_t * jnp.where(lab >= 0, 1.0, 0.0).astype(F32))
    gram_hi, gram_lo = split(dot(hi_v, hi) + dot(hi_v, lo) + dot(lo_v, hi))
    total = dot(w, gram_hi) + dot(w, gram_lo) - (dot(onehot, hi) + dot(onehot, lo))

    owners = part.shape[0] // 8
    part[pl.ds((owners - 1) * 8, 8)] = jnp.zeros((8, part.shape[1]), F32)
    part[pl.ds(0, classes)] = total

    def rows(o):
        return pl.ds(pl.multiple_of(o * 8, 8), 8)

    def term(k):
        to = (me + k) % devices
        return to, pltpu.make_async_remote_copy(
            src_ref=part.at[rows(to)], dst_ref=terms.at[k - 1], send_sem=s3.at[k - 1], recv_sem=r3.at[k - 1],
            device_id=device(to), device_id_type=MESH)

    def result(k):
        return pltpu.make_async_remote_copy(
            src_ref=summed.at[rows(me)], dst_ref=summed.at[rows(me)], send_sem=s4.at[k - 1], recv_sem=r4.at[me],
            device_id=device((me + k) % devices), device_id_type=MESH)

    def send_term(k, carry):
        to, copy = term(k)
        pl.when(to < owners)(copy.start)
        return carry
    lax.fori_loop(1, devices, send_term, 0)

    t_hi, t_lo = split(y_t)
    logits[...] = dot(w, t_hi) + dot(w, t_lo)

    @pl.when(me < owners)
    def _():
        def add(k, value):
            pltpu.make_async_remote_copy(
                src_ref=part.at[pl.ds(0, 8)], dst_ref=terms.at[k - 1], send_sem=s3.at[k - 1], recv_sem=r3.at[k - 1],
                device_id=device((me + k) % devices), device_id_type=MESH).wait_recv()
            return value + terms[k - 1]
        summed[rows(me)] = lax.fori_loop(1, devices, add, part[rows(me)])

        def send_result(k, carry):
            result(k).start()
            return carry
        lax.fori_loop(1, devices, send_result, 0)

    def take(o, carry):
        @pl.when(o != me)
        def _():
            pltpu.make_async_remote_copy(
                src_ref=summed.at[rows(o)], dst_ref=summed.at[rows(o)], send_sem=s4.at[0], recv_sem=r4.at[o],
                device_id=device((me + 1) % devices), device_id_type=MESH).wait_recv()
        return carry
    lax.fori_loop(0, owners, take, 0)
    wgrad[...] = summed[pl.ds(0, classes)] * scale

    def sent(k, carry):
        to, copy = term(k)
        pl.when(to < owners)(copy.wait_send)
        pl.when(me < owners)(result(k).wait_send)
        return carry
    lax.fori_loop(1, devices, sent, 0)


def local(n_row, n_col, features, weight, labels, tile_rows, tile_cols, tile_count, tile_vals):
    la, lb, cores = factors(n_row)
    classes, tile, slots = weight.shape[1], tile_vals.shape[-1], tile_vals.shape[2]
    own, feat = features.shape
    bt = own // tile
    rt, ct = n_col * bt, n_row * bt
    nodes = own * n_row * n_col
    key = jnp.where(jnp.arange(slots, dtype=jnp.int32) < tile_count.reshape(()),
                    tile_rows.reshape(slots) * ct + tile_cols.reshape(slots), -1)
    match = key[:, None] == jnp.arange(rt * ct, dtype=jnp.int32)[None, :]
    table = slots + jnp.sum(jnp.where(match, jnp.arange(slots, dtype=jnp.int32)[:, None] - slots, 0), axis=0)
    dims = (n_row, n_col, la, lb, cores, 1.0 / math.sqrt(nodes))
    vmem = pl.BlockSpec(memory_space=pltpu.VMEM)
    anywhere = pl.BlockSpec(memory_space=pl.ANY)
    dma = pltpu.SemaphoreType.DMA
    peers = max(1, n_col - 1)
    others = n_row * n_col - 1
    owners = -(-classes // 8)
    logits, wgrad = pl.pallas_call(
        functools.partial(kernel, dims),
        out_shape=(jax.ShapeDtypeStruct((classes, own), F32), jax.ShapeDtypeStruct((classes, feat), F32)),
        in_specs=[anywhere, vmem, vmem, pl.BlockSpec(memory_space=pltpu.SMEM), anywhere],
        out_specs=(vmem, vmem),
        scratch_shapes=[
            pltpu.VMEM((n_row, own, feat), BF16),
            pltpu.VMEM((slots + 1, tile, tile), BF16),
            pltpu.VMEM((rt, tile, feat), F32),
            pltpu.VMEM((rt, tile, feat), F32),
            pltpu.VMEM((peers, bt, tile, feat), BF16),
            pltpu.VMEM((peers, bt, tile, feat), F32),
            pltpu.VMEM((peers, bt, tile, feat), BF16),
            pltpu.VMEM((owners * 8, feat), F32),
            pltpu.VMEM((others, 8, feat), F32),
            pltpu.VMEM((owners * 8, feat), F32),
            dma((la * lb, 5)), dma((n_row,)), dma((4,)), dma(()),
            dma((peers,)), dma((peers,)), dma((peers,)), dma((peers,)),
            dma((others,)), dma((others,)), dma((others,)), dma((owners,)),
        ],
        compiler_params=pltpu.CompilerParams(collective_id=0, has_side_effects=True, vmem_limit_bytes=48 * 2**20),
        cost_estimate=pl.CostEstimate(flops=2 * rt * ct * tile * tile * feat, bytes_accessed=slots * tile * tile * 2, transcendentals=0),
        name="aggregate",
    )(features, weight.T, labels.reshape(1, own), table, tile_vals.reshape(slots, tile, tile))
    return logits.T, wgrad.T


def solution(mesh):
    placed = (
        P(("col", "row"), None),
        P(),
        P(("row", "col")),
        P("row", "col", None),
        P("row", "col", None),
        P("row", "col"),
        P("row", "col", None, None, None),
    )
    body = functools.partial(local, mesh.shape["row"], mesh.shape["col"])
    return jax.shard_map(
        body, mesh=mesh, in_specs=placed, out_specs=(P(("row", "col"), None), P()), check_vma=False
    )
```

```python
import functools
import math

import jax
import jax.numpy as jnp
from jax import lax
from jax.experimental import pallas as pl
from jax.experimental.pallas import tpu as pltpu
from jax.sharding import PartitionSpec as P

F32, BF16 = jnp.float32, jnp.bfloat16
MESH = pl.DeviceIdType.MESH


def factors(n_row):
    cores = 2 if n_row % 2 == 0 else 1
    chips = n_row // cores
    la = 4 if chips % 4 == 0 else chips
    return la, chips // la, cores


def nearest(pos, size, n):
    out = 0
    for p in range(size):
        order = sorted(range(size), key=lambda s: (abs(s - p), s))
        out = out + jnp.where(pos == p, order[n], 0)
    return out


def split(x):
    hi = x.astype(BF16)
    return hi, (x - hi.astype(F32)).astype(BF16)


def dot(a, b):
    return jnp.dot(a, b, preferred_element_type=F32)


def kernel(dims, feat, weight, labels, tab, vals, logits, wgrad,
           x, tiles, acc1, acc2, out2, in1, in2, part, terms, lined, summed, w_ref, lab_ref,
           ssem, rsem, vsem, fsem, s1, r1, s2, r2, s3, r3, s4, r4, s5, r5):
    n_row, n_col, la, lb, cores, scale = dims
    slots, tile = vals.shape[0], vals.shape[1]
    bt = feat.shape[0] // tile
    ct = n_row * bt
    row, col = lax.axis_index("row"), lax.axis_index("col")
    core = row % cores
    q = (row // cores) % lb
    p = row // (cores * lb)

    def place(s, t, c):
        return (s * lb + t) * cores + c

    def when(cond, fn):
        if cond is True:
            fn()
        else:
            pl.when(cond)(fn)

    size = lb * cores * n_col
    mine = (row % (lb * cores)) * n_col + col

    def device(place_a, index):
        return (place_a * (lb * cores) + index // n_col, index % n_col)

    own = pltpu.make_async_copy(feat, x.at[row], fsem.at[0])
    own.start()
    small = [pltpu.make_async_copy(weight, w_ref, fsem.at[1]), pltpu.make_async_copy(labels, lab_ref, fsem.at[2])]
    for copy in small:
        copy.start()
    pieces = vsem.shape[0]
    fetches = [pltpu.make_async_copy(vals.at[pl.ds(n * (slots // pieces), slots // pieces)],
                                     tiles.at[pl.ds(n * (slots // pieces), slots // pieces)], vsem.at[n])
               for n in range(pieces)]
    for copy in fetches:
        copy.start()

    def loop(n, body):
        def step(k, carry):
            body(k)
            return carry
        lax.fori_loop(1, n, step, 0, unroll=n <= 8)

    barrier = pltpu.get_barrier_semaphore()
    loop(size, lambda k: pl.semaphore_signal(barrier, inc=1, device_id=device(p, (mine + k) % size), device_id_type=MESH))
    loop(la, lambda k: pl.semaphore_signal(barrier, inc=1, device_id=device((p + k) % la, mine), device_id_type=MESH))
    tiles[slots] = jnp.zeros((tile, tile), BF16)
    own.wait()
    pl.semaphore_wait(barrier, size + la - 2)

    started = []

    def send(cond, step, way, block, where):
        copy = pltpu.make_async_remote_copy(
            src_ref=x.at[block], dst_ref=x.at[block], send_sem=ssem.at[step, way], recv_sem=rsem.at[block],
            device_id={"row": where}, device_id_type=MESH)
        when(cond, copy.start)
        started.append((cond, copy))

    def arrive(block):
        pltpu.make_async_remote_copy(
            src_ref=x.at[block], dst_ref=x.at[block], send_sem=ssem.at[0, 0], recv_sem=rsem.at[block],
            device_id={"row": (row + 1) % n_row}, device_id_type=MESH).wait_recv()

    def forward(na, nb, s, t):
        block, step = place(s, t, core), na * lb + nb
        if nb == 0:
            up = p + 1 < la if na == 0 else jnp.logical_and(s < p, p + 1 < la)
            down = p > 0 if na == 0 else jnp.logical_and(s > p, p > 0)
            send(up, step, 0, block, place(p + 1, q, core))
            send(down, step, 1, block, place(p - 1, q, core))
            send(q + 1 < lb, step, 2, block, place(p, q + 1, core))
            send(q > 0, step, 3, block, place(p, q - 1, core))
        elif lb > 2:
            send(jnp.logical_and(t < q, q + 1 < lb), step, 2, block, place(p, q + 1, core))
            send(jnp.logical_and(t > q, q > 0), step, 3, block, place(p, q - 1, core))
        if cores == 2:
            send(True, step, 4, block, place(p, q, 1 - core))

    def multiply(block, acc, lo, hi, first=False):
        def body(n, carry):
            chunk = (col + n) % n_col
            lines = []
            for i in range(bt):
                at = (chunk * bt + i) * ct + block * bt
                lines.append(jnp.concatenate([tiles[tab[at + m]] for m in range(bt)], axis=1))
            y = dot(jnp.concatenate(lines, axis=0), x[block]).reshape(bt, tile, acc1.shape[2])
            rows = pl.ds(chunk * bt, bt)
            acc[rows] = y if first else acc[rows] + y
            return carry
        lax.fori_loop(lo, hi, body, 0, unroll=2 if (hi - lo) % 2 == 0 else 1)

    groups = [[(step - nb, nb) for nb in range(lb) if 0 <= step - nb < la] for step in range(la + lb - 1)]
    early = max(1, len(groups) - 2)
    exchange1, exchange2 = [], []
    tail, todo = [], []
    for g, group in enumerate(groups):
        places = [(na, nb, nearest(p, la, na), nearest(q, lb, nb)) for na, nb in group]
        for na, nb, s, t in places:
            if g > 0:
                arrive(place(s, t, core))
            forward(na, nb, s, t)
        todo += [(place(s, t, core), False) for _, _, s, t in places]
        if cores == 2:
            todo += [(place(s, t, 1 - core), True) for _, _, s, t in places]
        if g == 0 and early > 1:
            continue
        if g == min(1, early - 1):
            for copy in fetches:
                copy.wait()
        acc = acc1 if g < early else acc2
        last = g == len(groups) - 1
        for n, (block, remote) in enumerate(todo):
            if remote:
                arrive(block)
            first = g in (min(1, early - 1), early) and n == 0
            if last:
                multiply(block, acc, 1, n_col, first)
                tail.append((block, first))
            else:
                multiply(block, acc, 1, n_col + 1, first)
        todo = []
        if g == early - 1:
            for k in range(1, n_col):
                to = (col + k) % n_col
                copy = pltpu.make_async_remote_copy(
                    src_ref=acc1.at[pl.ds(to * bt, bt)], dst_ref=in1.at[k - 1], send_sem=s1.at[k - 1],
                    recv_sem=r1.at[k - 1], device_id={"col": to}, device_id_type=MESH)
                copy.start()
                exchange1.append(copy)
    for k in range(1, n_col):
        to = (col + k) % n_col
        out2[k - 1] = acc2[pl.ds(to * bt, bt)].astype(BF16)
        copy = pltpu.make_async_remote_copy(
            src_ref=out2.at[k - 1], dst_ref=in2.at[k - 1], send_sem=s2.at[k - 1],
            recv_sem=r2.at[k - 1], device_id={"col": to}, device_id_type=MESH)
        copy.start()
        exchange2.append(copy)
    for block, first in tail:
        multiply(block, acc2, n_col, n_col + 1, first)
    for copy in small:
        copy.wait()
    w = w_ref[...]
    classes, feats = w.shape
    lab = lab_ref[...]
    onehot = (lax.broadcasted_iota(jnp.int32, (classes, bt * tile), 0) == lab).astype(F32).astype(BF16)
    valid = jnp.where(lab >= 0, 1.0, 0.0).astype(F32)
    y = acc1[pl.ds(col * bt, bt)] + acc2[pl.ds(col * bt, bt)]
    for n, copy in enumerate(exchange1):
        copy.wait()
        y = y + in1[n]
    y = y.reshape(bt * tile, feats)
    hi, lo = split(y)
    picked = dot(onehot, hi) + dot(onehot, lo)
    for n, copy in enumerate(exchange2):
        copy.wait()
        late = in2[n].reshape(bt * tile, feats)
        picked = picked + dot(onehot, late)
        y = y + late.astype(F32)
    hi, lo = split(y)
    y_t = y.T
    hi_v, lo_v = split(y_t * valid)
    gram_hi, gram_lo = split(dot(hi_v, hi) + dot(hi_v, lo) + dot(lo_v, hi))
    total = dot(w, gram_hi) + dot(w, gram_lo) - picked

    per = lined.shape[1]
    owners = part.shape[0] // per
    part[pl.ds((owners - 1) * per, per)] = jnp.zeros((per, feats), F32)
    part[pl.ds(0, classes)] = total

    def rows(o):
        return pl.ds(pl.multiple_of(o * per, per), per)

    def owner(o):
        return True if owners == size else o < owners

    def term(k, to):
        return pltpu.make_async_remote_copy(
            src_ref=part.at[rows(to)], dst_ref=terms.at[k - 1], send_sem=s3.at[k - 1], recv_sem=r3.at[k - 1],
            device_id=device(p, (mine + k) % size), device_id_type=MESH)

    def across(k, source):
        return pltpu.make_async_remote_copy(
            src_ref=lined.at[source], dst_ref=lined.at[source], send_sem=s4.at[k - 1], recv_sem=r4.at[source],
            device_id=device((p + k) % la, mine), device_id_type=MESH)

    def result(k, o):
        return pltpu.make_async_remote_copy(
            src_ref=summed.at[rows(o)], dst_ref=summed.at[rows(o)], send_sem=s5.at[k - 1], recv_sem=r5.at[o],
            device_id=device(p, (mine + k) % size), device_id_type=MESH)

    def send_term(k):
        to = (mine + k) % size
        when(owner(to), lambda: term(k, to).start())
    loop(size, send_term)

    t_hi, t_lo = split(y_t)
    logits[...] = dot(w, t_hi) + dot(w, t_lo)

    def reduce():
        def add(k, value):
            term(k, 0).wait_recv()
            return value + terms[k - 1]
        lined[p] = lax.fori_loop(1, size, add, part[rows(mine)], unroll=size <= 8)
        loop(la, lambda k: across(k, p).start())
        loop(la, lambda k: across(k, (p + k) % la).wait_recv())
        value = lined[0]
        for n in range(1, la):
            value = value + lined[n]
        summed[rows(mine)] = value
        loop(size, lambda k: result(k, mine).start())
    when(owner(mine), reduce)

    def take(k):
        o = (mine + k) % size
        when(owner(o), lambda: result(k, o).wait_recv())
    loop(size, take)
    wgrad[...] = summed[pl.ds(0, classes)] * scale

    for cond, copy in started:
        when(cond, copy.wait_send)

    def sent(k):
        to = (mine + k) % size
        when(owner(to), lambda: term(k, to).wait_send())
        when(owner(mine), lambda: result(k, mine).wait_send())
    loop(size, sent)
    when(owner(mine), lambda: loop(la, lambda k: across(k, p).wait_send()))


def local(n_row, n_col, features, weight, labels, tile_rows, tile_cols, tile_count, tile_vals):
    la, lb, cores = factors(n_row)
    classes, tile, slots = weight.shape[1], tile_vals.shape[-1], tile_vals.shape[2]
    own, feat = features.shape
    bt = own // tile
    rt, ct = n_col * bt, n_row * bt
    nodes = own * n_row * n_col
    key = jnp.where(jnp.arange(slots, dtype=jnp.int32) < tile_count.reshape(()),
                    tile_rows.reshape(slots) * ct + tile_cols.reshape(slots), -1)
    match = key[:, None] == jnp.arange(rt * ct, dtype=jnp.int32)[None, :]
    table = slots + jnp.sum(jnp.where(match, jnp.arange(slots, dtype=jnp.int32)[:, None] - slots, 0), axis=0)
    dims = (n_row, n_col, la, lb, cores, 1.0 / math.sqrt(nodes))
    vmem = pl.BlockSpec(memory_space=pltpu.VMEM)
    anywhere = pl.BlockSpec(memory_space=pl.ANY)
    dma = pltpu.SemaphoreType.DMA
    peers = max(1, n_col - 1)
    size = lb * cores * n_col
    chunks = -(-classes // 8)
    per = 8 * -(-chunks // size)
    owners = -(-chunks * 8 // per)
    logits, wgrad = pl.pallas_call(
        functools.partial(kernel, dims),
        out_shape=(jax.ShapeDtypeStruct((classes, own), F32), jax.ShapeDtypeStruct((classes, feat), F32)),
        in_specs=[anywhere, anywhere, anywhere, pl.BlockSpec(memory_space=pltpu.SMEM), anywhere],
        out_specs=(vmem, vmem),
        scratch_shapes=[
            pltpu.VMEM((n_row, own, feat), BF16),
            pltpu.VMEM((slots + 1, tile, tile), BF16),
            pltpu.VMEM((rt, tile, feat), F32),
            pltpu.VMEM((rt, tile, feat), F32),
            pltpu.VMEM((peers, bt, tile, feat), BF16),
            pltpu.VMEM((peers, bt, tile, feat), F32),
            pltpu.VMEM((peers, bt, tile, feat), BF16),
            pltpu.VMEM((owners * per, feat), F32),
            pltpu.VMEM((size - 1, per, feat), F32),
            pltpu.VMEM((la, per, feat), F32),
            pltpu.VMEM((owners * per, feat), F32),
            pltpu.VMEM((classes, feat), BF16),
            pltpu.VMEM((1, own), jnp.int32),
            dma((la * lb, 5)), dma((n_row,)), dma((4,)), dma((3,)),
            dma((peers,)), dma((peers,)), dma((peers,)), dma((peers,)),
            dma((size - 1,)), dma((size - 1,)), dma((la - 1,)), dma((la,)), dma((size - 1,)), dma((owners,)),
        ],
        compiler_params=pltpu.CompilerParams(collective_id=0, has_side_effects=True, vmem_limit_bytes=60 * 2**20),
        cost_estimate=pl.CostEstimate(flops=2 * rt * ct * tile * tile * feat, bytes_accessed=slots * tile * tile * 2, transcendentals=0),
        name="aggregate",
    )(features, weight.T, labels.reshape(1, own), table, tile_vals.reshape(slots, tile, tile))
    return logits.T, wgrad.T


def solution(mesh):
    placed = (
        P(("col", "row"), None),
        P(),
        P(("row", "col")),
        P("row", "col", None),
        P("row", "col", None),
        P("row", "col"),
        P("row", "col", None, None, None),
    )
    body = functools.partial(local, mesh.shape["row"], mesh.shape["col"])
    return jax.shard_map(
        body, mesh=mesh, in_specs=placed, out_specs=(P(("row", "col"), None), P()), check_vma=False
    )
```

```python
import functools
import math

import jax
import jax.numpy as jnp
from jax import lax
from jax.experimental import pallas as pl
from jax.experimental.pallas import tpu as pltpu
from jax.sharding import PartitionSpec as P

F32, BF16 = jnp.float32, jnp.bfloat16
MESH = pl.DeviceIdType.MESH


def factors(n_row):
    cores = 2 if n_row % 2 == 0 else 1
    chips = n_row // cores
    la = 4 if chips % 4 == 0 else chips
    return la, chips // la, cores


def nearest(pos, size, n):
    out = 0
    for p in range(size):
        order = sorted(range(size), key=lambda s: (abs(s - p), s))
        out = out + jnp.where(pos == p, order[n], 0)
    return out


def split(x):
    hi = x.astype(BF16)
    return hi, (x - hi.astype(F32)).astype(BF16)


def dot(a, b):
    return jnp.dot(a, b, preferred_element_type=F32)


def kernel(dims, feat, weight, labels, tab, vals, logits, wgrad,
           x, tiles, acc1, acc2, out2, in1, in2, part, terms, lined, summed, w_ref, lab_ref,
           ssem, rsem, vsem, fsem, s1, r1, s2, r2, s3, r3, s4, r4, s5, r5):
    n_row, n_col, la, lb, cores, scale = dims
    slots, tile = vals.shape[0], vals.shape[1]
    bt = feat.shape[0] // tile
    ct = n_row * bt
    row, col = lax.axis_index("row"), lax.axis_index("col")
    core = row % cores
    q = (row // cores) % lb
    p = row // (cores * lb)

    def place(s, t, c):
        return (s * lb + t) * cores + c

    def when(cond, fn):
        if cond is True:
            fn()
        else:
            pl.when(cond)(fn)

    size = lb * cores * n_col
    mine = (row % (lb * cores)) * n_col + col

    def device(place_a, index):
        return (place_a * (lb * cores) + index // n_col, index % n_col)

    own = pltpu.make_async_copy(feat, x.at[row], fsem.at[0])
    own.start()
    small = [pltpu.make_async_copy(weight, w_ref, fsem.at[1]), pltpu.make_async_copy(labels, lab_ref, fsem.at[2])]
    for copy in small:
        copy.start()
    pieces = vsem.shape[0]
    fetches = [pltpu.make_async_copy(vals.at[pl.ds(n * (slots // pieces), slots // pieces)],
                                     tiles.at[pl.ds(n * (slots // pieces), slots // pieces)], vsem.at[n])
               for n in range(pieces)]
    for copy in fetches:
        copy.start()

    def loop(n, body):
        def step(k, carry):
            body(k)
            return carry
        lax.fori_loop(1, n, step, 0, unroll=n <= 8)

    barrier = pltpu.get_barrier_semaphore()
    loop(size, lambda k: pl.semaphore_signal(barrier, inc=1, device_id=device(p, (mine + k) % size), device_id_type=MESH))
    loop(la, lambda k: pl.semaphore_signal(barrier, inc=1, device_id=device((p + k) % la, mine), device_id_type=MESH))
    tiles[slots] = jnp.zeros((tile, tile), BF16)
    own.wait()
    pl.semaphore_wait(barrier, size + la - 2)

    started = []

    def send(cond, step, way, block, where):
        copy = pltpu.make_async_remote_copy(
            src_ref=x.at[block], dst_ref=x.at[block], send_sem=ssem.at[step, way], recv_sem=rsem.at[block],
            device_id={"row": where}, device_id_type=MESH)
        when(cond, copy.start)
        started.append((cond, copy))

    def arrive(block):
        pltpu.make_async_remote_copy(
            src_ref=x.at[block], dst_ref=x.at[block], send_sem=ssem.at[0, 0], recv_sem=rsem.at[block],
            device_id={"row": (row + 1) % n_row}, device_id_type=MESH).wait_recv()

    def forward(na, nb, s, t):
        block, step = place(s, t, core), na * lb + nb
        if na == 0 and nb == 0:
            for n in range(1, la):
                send(True, step, 4 + n, block, place(nearest(p, la, n), q, core))
        if nb == 0:
            send(q + 1 < lb, step, 2, block, place(p, q + 1, core))
            send(q > 0, step, 3, block, place(p, q - 1, core))
        elif lb > 2:
            send(jnp.logical_and(t < q, q + 1 < lb), step, 2, block, place(p, q + 1, core))
            send(jnp.logical_and(t > q, q > 0), step, 3, block, place(p, q - 1, core))
        if cores == 2:
            send(True, step, 4, block, place(p, q, 1 - core))

    def multiply(block, acc, lo, hi, first=False):
        def body(n, carry):
            chunk = (col + n) % n_col
            half = max(1, bt // 2)
            for i in range(0, bt, half):
                lines = []
                for m in range(i, i + half):
                    at = (chunk * bt + m) * ct + block * bt
                    lines.append(jnp.concatenate([tiles[tab[at + j]] for j in range(bt)], axis=1))
                y = dot(jnp.concatenate(lines, axis=0), x[block]).reshape(half, tile, acc1.shape[2])
                rows = pl.ds(chunk * bt + i, half)
                acc[rows] = y if first else acc[rows] + y
            return carry
        lax.fori_loop(lo, hi, body, 0, unroll=2 if (hi - lo) % 2 == 0 else 1)

    groups = [[(step - nb, nb) for nb in range(lb) if 0 <= step - nb < la] for step in range(la + lb - 1)]
    early = max(1, len(groups) - 3)
    exchange1, exchange2 = [], []
    tail, begun = [], []
    where = [[(na, nb, nearest(p, la, na), nearest(q, lb, nb)) for na, nb in group] for group in groups]

    def pass_on(g):
        for na, nb, s, t in where[g]:
            if g > 0:
                arrive(place(s, t, core))
            forward(na, nb, s, t)

    def compute(g, sibling):
        acc = acc1 if g < early else acc2
        for _, _, s, t in where[g]:
            block = place(s, t, 1 - core if sibling else core)
            if sibling:
                arrive(block)
            first = not any(acc is other for other in begun)
            begun.append(acc)
            if g == len(groups) - 1:
                multiply(block, acc, 1, n_col, first)
                tail.append((block, first))
            else:
                multiply(block, acc, 1, n_col + 1, first)

    pass_on(0)
    for g in range(len(groups)):
        if g == 0 and len(groups) > 1:
            pass_on(1)
        if g == 0:
            for copy in fetches:
                copy.wait()
        compute(g, False)
        if 0 < g < len(groups) - 2:
            pass_on(g + 1)
        if cores == 2:
            compute(g, True)
        if 0 < g == len(groups) - 2:
            pass_on(g + 1)
        if g == early - 1:
            for k in range(1, n_col):
                to = (col + k) % n_col
                copy = pltpu.make_async_remote_copy(
                    src_ref=acc1.at[pl.ds(to * bt, bt)], dst_ref=in1.at[k - 1], send_sem=s1.at[k - 1],
                    recv_sem=r1.at[k - 1], device_id={"col": to}, device_id_type=MESH)
                copy.start()
                exchange1.append(copy)
    for k in range(1, n_col):
        to = (col + k) % n_col
        out2[k - 1] = acc2[pl.ds(to * bt, bt)].astype(BF16)
        copy = pltpu.make_async_remote_copy(
            src_ref=out2.at[k - 1], dst_ref=in2.at[k - 1], send_sem=s2.at[k - 1],
            recv_sem=r2.at[k - 1], device_id={"col": to}, device_id_type=MESH)
        copy.start()
        exchange2.append(copy)
    for block, first in tail:
        multiply(block, acc2, n_col, n_col + 1, first)
    for copy in small:
        copy.wait()
    w = w_ref[...]
    classes, feats = w.shape
    lab = lab_ref[...]
    onehot = (lax.broadcasted_iota(jnp.int32, (classes, bt * tile), 0) == lab).astype(F32).astype(BF16)
    valid = jnp.where(lab >= 0, 1.0, 0.0).astype(F32)
    y = acc1[pl.ds(col * bt, bt)] + acc2[pl.ds(col * bt, bt)]
    for n, copy in enumerate(exchange1):
        copy.wait()
        y = y + in1[n]
    y = y.reshape(bt * tile, feats)
    hi, lo = split(y)
    picked = dot(onehot, hi) + dot(onehot, lo)
    for n, copy in enumerate(exchange2):
        copy.wait()
        late = in2[n].reshape(bt * tile, feats)
        picked = picked + dot(onehot, late)
        y = y + late.astype(F32)
    hi, lo = split(y)
    y_t = y.T
    hi_v, lo_v = split(y_t * valid)
    gram_hi, gram_lo = split(dot(hi_v, hi) + dot(hi_v, lo) + dot(lo_v, hi))
    total = dot(w, gram_hi) + dot(w, gram_lo) - picked

    per = lined.shape[1]
    owners = part.shape[0] // per
    part[pl.ds((owners - 1) * per, per)] = jnp.zeros((per, feats), F32)
    part[pl.ds(0, classes)] = total

    def rows(o):
        return pl.ds(pl.multiple_of(o * per, per), per)

    def owner(o):
        return True if owners == size else o < owners

    def term(k, to):
        return pltpu.make_async_remote_copy(
            src_ref=part.at[rows(to)], dst_ref=terms.at[k - 1], send_sem=s3.at[k - 1], recv_sem=r3.at[k - 1],
            device_id=device(p, (mine + k) % size), device_id_type=MESH)

    def across(k, source):
        return pltpu.make_async_remote_copy(
            src_ref=lined.at[source], dst_ref=lined.at[source], send_sem=s4.at[k - 1], recv_sem=r4.at[source],
            device_id=device((p + k) % la, mine), device_id_type=MESH)

    def result(k, o):
        return pltpu.make_async_remote_copy(
            src_ref=summed.at[rows(o)], dst_ref=summed.at[rows(o)], send_sem=s5.at[k - 1], recv_sem=r5.at[o],
            device_id=device(p, (mine + k) % size), device_id_type=MESH)

    def send_term(k):
        to = (mine + k) % size
        when(owner(to), lambda: term(k, to).start())
    loop(size, send_term)

    t_hi, t_lo = split(y_t)
    logits[...] = dot(w, t_hi) + dot(w, t_lo)

    def reduce():
        def add(k, value):
            term(k, 0).wait_recv()
            return value + terms[k - 1]
        lined[p] = lax.fori_loop(1, size, add, part[rows(mine)], unroll=size <= 8)
        loop(la, lambda k: across(k, p).start())
        loop(la, lambda k: across(k, (p + k) % la).wait_recv())
        value = lined[0]
        for n in range(1, la):
            value = value + lined[n]
        summed[rows(mine)] = value
        loop(size, lambda k: result(k, mine).start())
    when(owner(mine), reduce)

    def take(k):
        o = (mine + k) % size
        when(owner(o), lambda: result(k, o).wait_recv())
    loop(size, take)
    wgrad[...] = summed[pl.ds(0, classes)] * scale

    for cond, copy in started:
        when(cond, copy.wait_send)

    def sent(k):
        to = (mine + k) % size
        when(owner(to), lambda: term(k, to).wait_send())
        when(owner(mine), lambda: result(k, mine).wait_send())
    loop(size, sent)
    when(owner(mine), lambda: loop(la, lambda k: across(k, p).wait_send()))


def local(n_row, n_col, features, weight, labels, tile_rows, tile_cols, tile_count, tile_vals):
    la, lb, cores = factors(n_row)
    classes, tile, slots = weight.shape[1], tile_vals.shape[-1], tile_vals.shape[2]
    own, feat = features.shape
    bt = own // tile
    rt, ct = n_col * bt, n_row * bt
    nodes = own * n_row * n_col
    key = jnp.where(jnp.arange(slots, dtype=jnp.int32) < tile_count.reshape(()),
                    tile_rows.reshape(slots) * ct + tile_cols.reshape(slots), -1)
    match = key[:, None] == jnp.arange(rt * ct, dtype=jnp.int32)[None, :]
    table = slots + jnp.sum(jnp.where(match, jnp.arange(slots, dtype=jnp.int32)[:, None] - slots, 0), axis=0)
    dims = (n_row, n_col, la, lb, cores, 1.0 / math.sqrt(nodes))
    vmem = pl.BlockSpec(memory_space=pltpu.VMEM)
    anywhere = pl.BlockSpec(memory_space=pl.ANY)
    dma = pltpu.SemaphoreType.DMA
    peers = max(1, n_col - 1)
    size = lb * cores * n_col
    chunks = -(-classes // 8)
    per = 8 * -(-chunks // size)
    owners = -(-chunks * 8 // per)
    logits, wgrad = pl.pallas_call(
        functools.partial(kernel, dims),
        out_shape=(jax.ShapeDtypeStruct((classes, own), F32), jax.ShapeDtypeStruct((classes, feat), F32)),
        in_specs=[anywhere, anywhere, anywhere, pl.BlockSpec(memory_space=pltpu.SMEM), anywhere],
        out_specs=(vmem, vmem),
        scratch_shapes=[
            pltpu.VMEM((n_row, own, feat), BF16),
            pltpu.VMEM((slots + 1, tile, tile), BF16),
            pltpu.VMEM((rt, tile, feat), F32),
            pltpu.VMEM((rt, tile, feat), F32),
            pltpu.VMEM((peers, bt, tile, feat), BF16),
            pltpu.VMEM((peers, bt, tile, feat), F32),
            pltpu.VMEM((peers, bt, tile, feat), BF16),
            pltpu.VMEM((owners * per, feat), F32),
            pltpu.VMEM((size - 1, per, feat), F32),
            pltpu.VMEM((la, per, feat), F32),
            pltpu.VMEM((owners * per, feat), F32),
            pltpu.VMEM((classes, feat), BF16),
            pltpu.VMEM((1, own), jnp.int32),
            dma((la * lb, 4 + la)), dma((n_row,)), dma((4,)), dma((3,)),
            dma((peers,)), dma((peers,)), dma((peers,)), dma((peers,)),
            dma((size - 1,)), dma((size - 1,)), dma((la - 1,)), dma((la,)), dma((size - 1,)), dma((owners,)),
        ],
        compiler_params=pltpu.CompilerParams(collective_id=0, has_side_effects=True, vmem_limit_bytes=48 * 2**20),
        cost_estimate=pl.CostEstimate(flops=2 * rt * ct * tile * tile * feat, bytes_accessed=slots * tile * tile * 2, transcendentals=0),
        name="aggregate",
    )(features, weight.T, labels.reshape(1, own), table, tile_vals.reshape(slots, tile, tile))
    return logits.T, wgrad.T


def solution(mesh):
    placed = (
        P(("col", "row"), None),
        P(),
        P(("row", "col")),
        P("row", "col", None),
        P("row", "col", None),
        P("row", "col"),
        P("row", "col", None, None, None),
    )
    body = functools.partial(local, mesh.shape["row"], mesh.shape["col"])
    return jax.shard_map(
        body, mesh=mesh, in_specs=placed, out_specs=(P(("row", "col"), None), P()), check_vma=False
    )
```

```python
import functools
import math

import jax
import jax.numpy as jnp
from jax import lax
from jax.experimental import pallas as pl
from jax.experimental.pallas import tpu as pltpu
from jax.sharding import PartitionSpec as P

F32, BF16 = jnp.float32, jnp.bfloat16
MESH = pl.DeviceIdType.MESH


def factors(n_row):
    cores = 2 if n_row % 2 == 0 else 1
    chips = n_row // cores
    la = 4 if chips % 4 == 0 else chips
    return la, chips // la, cores


def nearest(pos, size, n):
    out = 0
    for p in range(size):
        order = sorted(range(size), key=lambda s: (abs(s - p), s))
        out = out + jnp.where(pos == p, order[n], 0)
    return out


def split(x):
    hi = x.astype(BF16)
    return hi, (x - hi.astype(F32)).astype(BF16)


def dot(a, b):
    return jnp.dot(a, b, preferred_element_type=F32)


def kernel(dims, feat, weight, labels, tab, vals, logits, wgrad,
           x, tiles, acc1, acc2, out2, in1, in2, part, terms, lined, summed, w_ref, lab_ref,
           ssem, rsem, vsem, fsem, s1, r1, s2, r2, s3, r3, s4, r4, s5, r5):
    n_row, n_col, la, lb, cores, scale = dims
    slots, tile = vals.shape[0], vals.shape[1]
    bt = feat.shape[0] // tile
    ct = n_row * bt
    row, col = lax.axis_index("row"), lax.axis_index("col")
    core = row % cores
    q = (row // cores) % lb
    p = row // (cores * lb)

    def place(s, t, c):
        return (s * lb + t) * cores + c

    def when(cond, fn):
        if cond is True:
            fn()
        else:
            pl.when(cond)(fn)

    size = lb * cores * n_col
    mine = (row % (lb * cores)) * n_col + col

    def device(place_a, index):
        return (place_a * (lb * cores) + index // n_col, index % n_col)

    own = pltpu.make_async_copy(feat, x.at[row], fsem.at[0])
    own.start()
    small = [pltpu.make_async_copy(weight, w_ref, fsem.at[1]), pltpu.make_async_copy(labels, lab_ref, fsem.at[2])]
    for copy in small:
        copy.start()
    pieces = vsem.shape[0]
    fetches = [pltpu.make_async_copy(vals.at[pl.ds(n * (slots // pieces), slots // pieces)],
                                     tiles.at[pl.ds(n * (slots // pieces), slots // pieces)], vsem.at[n])
               for n in range(pieces)]
    for copy in fetches:
        copy.start()

    def loop(n, body):
        def step(k, carry):
            body(k)
            return carry
        lax.fori_loop(1, n, step, 0, unroll=n <= 8)

    barrier = pltpu.get_barrier_semaphore()
    loop(size, lambda k: pl.semaphore_signal(barrier, inc=1, device_id=device(p, (mine + k) % size), device_id_type=MESH))
    loop(la, lambda k: pl.semaphore_signal(barrier, inc=1, device_id=device((p + k) % la, mine), device_id_type=MESH))
    acc1[...] = jnp.zeros_like(acc1)
    acc2[...] = jnp.zeros_like(acc2)
    tiles[slots] = jnp.zeros((tile, tile), BF16)
    own.wait()
    pl.semaphore_wait(barrier, size + la - 2)

    started = []

    def send(cond, step, way, block, where):
        copy = pltpu.make_async_remote_copy(
            src_ref=x.at[block], dst_ref=x.at[block], send_sem=ssem.at[step, way], recv_sem=rsem.at[block],
            device_id={"row": where}, device_id_type=MESH)
        when(cond, copy.start)
        started.append((cond, copy))

    def arrive(block):
        pltpu.make_async_remote_copy(
            src_ref=x.at[block], dst_ref=x.at[block], send_sem=ssem.at[0, 0], recv_sem=rsem.at[block],
            device_id={"row": (row + 1) % n_row}, device_id_type=MESH).wait_recv()

    def forward(na, nb, s, t):
        block, step = place(s, t, core), na * lb + nb
        if nb == 0:
            up = p + 1 < la if na == 0 else jnp.logical_and(s < p, p + 1 < la)
            down = p > 0 if na == 0 else jnp.logical_and(s > p, p > 0)
            send(up, step, 0, block, place(p + 1, q, core))
            send(down, step, 1, block, place(p - 1, q, core))
            send(q + 1 < lb, step, 2, block, place(p, q + 1, core))
            send(q > 0, step, 3, block, place(p, q - 1, core))
        elif lb > 2:
            send(jnp.logical_and(t < q, q + 1 < lb), step, 2, block, place(p, q + 1, core))
            send(jnp.logical_and(t > q, q > 0), step, 3, block, place(p, q - 1, core))
        if cores == 2:
            send(True, step, 4, block, place(p, q, 1 - core))

    def multiply(blocks, passed, acc, lo, hi):
        def body(e, carry):
            block = 0
            for n, b in enumerate(blocks):
                block = block + jnp.where(e == n, b, 0)
            pl.when(e >= passed)(lambda: arrive(block))

            def rows(n, carry):
                chunk = (col + n) % n_col
                lines = []
                for i in range(bt):
                    at = (chunk * bt + i) * ct + block * bt
                    lines.append(jnp.concatenate([tiles[tab[at + m]] for m in range(bt)], axis=1))
                y = dot(jnp.concatenate(lines, axis=0), x[block]).reshape(bt, tile, acc1.shape[2])
                acc[pl.ds(chunk * bt, bt)] += y
                return carry
            return lax.fori_loop(lo, hi, rows, carry)
        lax.fori_loop(0, len(blocks), body, 0)

    groups = [[(step - nb, nb) for nb in range(lb) if 0 <= step - nb < la] for step in range(la + lb - 1)]
    early = max(1, len(groups) - 2)
    exchange1, exchange2 = [], []
    tail, todo = [], []
    for g, group in enumerate(groups):
        places = [(na, nb, nearest(p, la, na), nearest(q, lb, nb)) for na, nb in group]
        for na, nb, s, t in places:
            if g > 0:
                arrive(place(s, t, core))
            forward(na, nb, s, t)
        todo += [(place(s, t, core), False) for _, _, s, t in places]
        if cores == 2:
            todo += [(place(s, t, 1 - core), True) for _, _, s, t in places]
        if g == 0 and early > 1:
            continue
        if g == min(1, early - 1):
            for copy in fetches:
                copy.wait()
        acc = acc1 if g < early else acc2
        last = g == len(groups) - 1
        todo.sort(key=lambda entry: entry[1])
        blocks = [block for block, _ in todo]
        passed = sum(not remote for _, remote in todo)
        multiply(blocks, passed, acc, 1, n_col if last else n_col + 1)
        if last:
            tail = blocks
        todo = []
        if g == early - 1:
            for k in range(1, n_col):
                to = (col + k) % n_col
                copy = pltpu.make_async_remote_copy(
                    src_ref=acc1.at[pl.ds(to * bt, bt)], dst_ref=in1.at[k - 1], send_sem=s1.at[k - 1],
                    recv_sem=r1.at[k - 1], device_id={"col": to}, device_id_type=MESH)
                copy.start()
                exchange1.append(copy)
    for k in range(1, n_col):
        to = (col + k) % n_col
        out2[k - 1] = acc2[pl.ds(to * bt, bt)].astype(BF16)
        copy = pltpu.make_async_remote_copy(
            src_ref=out2.at[k - 1], dst_ref=in2.at[k - 1], send_sem=s2.at[k - 1],
            recv_sem=r2.at[k - 1], device_id={"col": to}, device_id_type=MESH)
        copy.start()
        exchange2.append(copy)
    multiply(tail, len(tail), acc2, n_col, n_col + 1)
    for copy in small:
        copy.wait()
    w = w_ref[...]
    classes, feats = w.shape
    lab = lab_ref[...]
    onehot = (lax.broadcasted_iota(jnp.int32, (classes, bt * tile), 0) == lab).astype(F32).astype(BF16)
    valid = jnp.where(lab >= 0, 1.0, 0.0).astype(F32)
    y = acc1[pl.ds(col * bt, bt)] + acc2[pl.ds(col * bt, bt)]
    for n, copy in enumerate(exchange1):
        copy.wait()
        y = y + in1[n]
    y = y.reshape(bt * tile, feats)
    hi, lo = split(y)
    picked = dot(onehot, hi) + dot(onehot, lo)
    for n, copy in enumerate(exchange2):
        copy.wait()
        late = in2[n].reshape(bt * tile, feats)
        picked = picked + dot(onehot, late)
        y = y + late.astype(F32)
    hi, lo = split(y)
    y_t = y.T
    hi_v, lo_v = split(y_t * valid)
    gram_hi, gram_lo = split(dot(hi_v, hi) + dot(hi_v, lo) + dot(lo_v, hi))
    total = dot(w, gram_hi) + dot(w, gram_lo) - picked

    per = lined.shape[1]
    owners = part.shape[0] // per
    part[pl.ds((owners - 1) * per, per)] = jnp.zeros((per, feats), F32)
    part[pl.ds(0, classes)] = total

    def rows(o):
        return pl.ds(pl.multiple_of(o * per, per), per)

    def owner(o):
        return True if owners == size else o < owners

    def term(k, to):
        return pltpu.make_async_remote_copy(
            src_ref=part.at[rows(to)], dst_ref=terms.at[k - 1], send_sem=s3.at[k - 1], recv_sem=r3.at[k - 1],
            device_id=device(p, (mine + k) % size), device_id_type=MESH)

    def across(k, source):
        return pltpu.make_async_remote_copy(
            src_ref=lined.at[source], dst_ref=lined.at[source], send_sem=s4.at[k - 1], recv_sem=r4.at[source],
            device_id=device((p + k) % la, mine), device_id_type=MESH)

    def result(k, o):
        return pltpu.make_async_remote_copy(
            src_ref=summed.at[rows(o)], dst_ref=summed.at[rows(o)], send_sem=s5.at[k - 1], recv_sem=r5.at[o],
            device_id=device(p, (mine + k) % size), device_id_type=MESH)

    def send_term(k):
        to = (mine + k) % size
        when(owner(to), lambda: term(k, to).start())
    loop(size, send_term)

    t_hi, t_lo = split(y_t)
    logits[...] = dot(w, t_hi) + dot(w, t_lo)

    def reduce():
        def add(k, value):
            term(k, 0).wait_recv()
            return value + terms[k - 1]
        lined[p] = lax.fori_loop(1, size, add, part[rows(mine)], unroll=size <= 8)
        loop(la, lambda k: across(k, p).start())
        loop(la, lambda k: across(k, (p + k) % la).wait_recv())
        value = lined[0]
        for n in range(1, la):
            value = value + lined[n]
        summed[rows(mine)] = value
        loop(size, lambda k: result(k, mine).start())
    when(owner(mine), reduce)

    def take(k):
        o = (mine + k) % size
        when(owner(o), lambda: result(k, o).wait_recv())
    loop(size, take)
    wgrad[...] = summed[pl.ds(0, classes)] * scale

    for cond, copy in started:
        when(cond, copy.wait_send)

    def sent(k):
        to = (mine + k) % size
        when(owner(to), lambda: term(k, to).wait_send())
        when(owner(mine), lambda: result(k, mine).wait_send())
    loop(size, sent)
    when(owner(mine), lambda: loop(la, lambda k: across(k, p).wait_send()))


def local(n_row, n_col, features, weight, labels, tile_rows, tile_cols, tile_count, tile_vals):
    la, lb, cores = factors(n_row)
    classes, tile, slots = weight.shape[1], tile_vals.shape[-1], tile_vals.shape[2]
    own, feat = features.shape
    bt = own // tile
    rt, ct = n_col * bt, n_row * bt
    nodes = own * n_row * n_col
    key = jnp.where(jnp.arange(slots, dtype=jnp.int32) < tile_count.reshape(()),
                    tile_rows.reshape(slots) * ct + tile_cols.reshape(slots), -1)
    match = key[:, None] == jnp.arange(rt * ct, dtype=jnp.int32)[None, :]
    table = slots + jnp.sum(jnp.where(match, jnp.arange(slots, dtype=jnp.int32)[:, None] - slots, 0), axis=0)
    dims = (n_row, n_col, la, lb, cores, 1.0 / math.sqrt(nodes))
    vmem = pl.BlockSpec(memory_space=pltpu.VMEM)
    anywhere = pl.BlockSpec(memory_space=pl.ANY)
    dma = pltpu.SemaphoreType.DMA
    peers = max(1, n_col - 1)
    size = lb * cores * n_col
    chunks = -(-classes // 8)
    per = 8 * -(-chunks // size)
    owners = -(-chunks * 8 // per)
    logits, wgrad = pl.pallas_call(
        functools.partial(kernel, dims),
        out_shape=(jax.ShapeDtypeStruct((classes, own), F32), jax.ShapeDtypeStruct((classes, feat), F32)),
        in_specs=[anywhere, anywhere, anywhere, pl.BlockSpec(memory_space=pltpu.SMEM), anywhere],
        out_specs=(vmem, vmem),
        scratch_shapes=[
            pltpu.VMEM((n_row, own, feat), BF16),
            pltpu.VMEM((slots + 1, tile, tile), BF16),
            pltpu.VMEM((rt, tile, feat), F32),
            pltpu.VMEM((rt, tile, feat), F32),
            pltpu.VMEM((peers, bt, tile, feat), BF16),
            pltpu.VMEM((peers, bt, tile, feat), F32),
            pltpu.VMEM((peers, bt, tile, feat), BF16),
            pltpu.VMEM((owners * per, feat), F32),
            pltpu.VMEM((size - 1, per, feat), F32),
            pltpu.VMEM((la, per, feat), F32),
            pltpu.VMEM((owners * per, feat), F32),
            pltpu.VMEM((classes, feat), BF16),
            pltpu.VMEM((1, own), jnp.int32),
            dma((la * lb, 5)), dma((n_row,)), dma((4,)), dma((3,)),
            dma((peers,)), dma((peers,)), dma((peers,)), dma((peers,)),
            dma((size - 1,)), dma((size - 1,)), dma((la - 1,)), dma((la,)), dma((size - 1,)), dma((owners,)),
        ],
        compiler_params=pltpu.CompilerParams(collective_id=0, has_side_effects=True, vmem_limit_bytes=60 * 2**20),
        cost_estimate=pl.CostEstimate(flops=2 * rt * ct * tile * tile * feat, bytes_accessed=slots * tile * tile * 2, transcendentals=0),
        name="aggregate",
    )(features, weight.T, labels.reshape(1, own), table, tile_vals.reshape(slots, tile, tile))
    return logits.T, wgrad.T


def solution(mesh):
    placed = (
        P(("col", "row"), None),
        P(),
        P(("row", "col")),
        P("row", "col", None),
        P("row", "col", None),
        P("row", "col"),
        P("row", "col", None, None, None),
    )
    body = functools.partial(local, mesh.shape["row"], mesh.shape["col"])
    return jax.shard_map(
        body, mesh=mesh, in_specs=placed, out_specs=(P(("row", "col"), None), P()), check_vma=False
    )
```

```python
import functools
import math

import jax
import jax.numpy as jnp
from jax import lax
from jax.experimental import pallas as pl
from jax.experimental.pallas import tpu as pltpu
from jax.sharding import PartitionSpec as P

F32, BF16 = jnp.float32, jnp.bfloat16
MESH = pl.DeviceIdType.MESH


def factors(n_row):
    cores = 2 if n_row % 2 == 0 else 1
    chips = n_row // cores
    la = 4 if chips % 4 == 0 else chips
    return la, chips // la, cores


def nearest(pos, size, n):
    out = 0
    for p in range(size):
        order = sorted(range(size), key=lambda s: (abs(s - p), s))
        out = out + jnp.where(pos == p, order[n], 0)
    return out


def split(x):
    hi = x.astype(BF16)
    return hi, (x - hi.astype(F32)).astype(BF16)


def dot(a, b):
    return jnp.dot(a, b, preferred_element_type=F32)


def kernel(dims, feat, weight, labels, tab, vals, logits, wgrad,
           x, tiles, acc1, acc2, out2, in1, in2, part, terms, lined, summed, w_ref, lab_ref,
           ssem, rsem, vsem, fsem, s1, r1, s2, r2, s3, r3, s4, r4, s5, r5):
    n_row, n_col, la, lb, cores, scale = dims
    slots, tile = vals.shape[0], vals.shape[1]
    bt = feat.shape[0] // tile
    ct = n_row * bt
    row, col = lax.axis_index("row"), lax.axis_index("col")
    core = row % cores
    q = (row // cores) % lb
    p = row // (cores * lb)

    def place(s, t, c):
        return (s * lb + t) * cores + c

    def when(cond, fn):
        if cond is True:
            fn()
        else:
            pl.when(cond)(fn)

    size = lb * cores * n_col
    mine = (row % (lb * cores)) * n_col + col

    def device(place_a, index):
        return (place_a * (lb * cores) + index // n_col, index % n_col)

    own = pltpu.make_async_copy(feat, x.at[row], fsem.at[0])
    own.start()
    small = [pltpu.make_async_copy(weight, w_ref, fsem.at[1]), pltpu.make_async_copy(labels, lab_ref, fsem.at[2])]
    for copy in small:
        copy.start()
    pieces = vsem.shape[0]
    fetches = [pltpu.make_async_copy(vals.at[pl.ds(n * (slots // pieces), slots // pieces)],
                                     tiles.at[pl.ds(n * (slots // pieces), slots // pieces)], vsem.at[n])
               for n in range(pieces)]

    def loop(n, body):
        def step(k, carry):
            body(k)
            return carry
        lax.fori_loop(1, n, step, 0, unroll=n <= 8)

    barrier = pltpu.get_barrier_semaphore()
    loop(size, lambda k: pl.semaphore_signal(barrier, inc=1, device_id=device(p, (mine + k) % size), device_id_type=MESH))
    loop(la, lambda k: pl.semaphore_signal(barrier, inc=1, device_id=device((p + k) % la, mine), device_id_type=MESH))
    tiles[slots] = jnp.zeros((tile, tile), BF16)
    own.wait()
    pl.semaphore_wait(barrier, size + la - 2)

    started = []

    def send(cond, step, way, block, where):
        copy = pltpu.make_async_remote_copy(
            src_ref=x.at[block], dst_ref=x.at[block], send_sem=ssem.at[step, way], recv_sem=rsem.at[block],
            device_id={"row": where}, device_id_type=MESH)
        when(cond, copy.start)
        started.append((cond, copy))

    def arrive(block):
        pltpu.make_async_remote_copy(
            src_ref=x.at[block], dst_ref=x.at[block], send_sem=ssem.at[0, 0], recv_sem=rsem.at[block],
            device_id={"row": (row + 1) % n_row}, device_id_type=MESH).wait_recv()

    def forward(na, nb, s, t):
        block, step = place(s, t, core), na * lb + nb
        if nb == 0:
            up = p + 1 < la if na == 0 else jnp.logical_and(s < p, p + 1 < la)
            down = p > 0 if na == 0 else jnp.logical_and(s > p, p > 0)
            send(up, step, 0, block, place(p + 1, q, core))
            send(down, step, 1, block, place(p - 1, q, core))
            send(q + 1 < lb, step, 2, block, place(p, q + 1, core))
            send(q > 0, step, 3, block, place(p, q - 1, core))
        elif lb > 2:
            send(jnp.logical_and(t < q, q + 1 < lb), step, 2, block, place(p, q + 1, core))
            send(jnp.logical_and(t > q, q > 0), step, 3, block, place(p, q - 1, core))
        if cores == 2:
            send(True, step, 4, block, place(p, q, 1 - core))

    def multiply(block, acc, lo, hi, first=False):
        def body(n, carry):
            chunk = (col + n) % n_col
            lines = []
            for i in range(bt):
                at = (chunk * bt + i) * ct + block * bt
                lines.append(jnp.concatenate([tiles[tab[at + m]] for m in range(bt)], axis=1))
            y = dot(jnp.concatenate(lines, axis=0), x[block]).reshape(bt, tile, acc1.shape[2])
            rows = pl.ds(chunk * bt, bt)
            acc[rows] = y if first else acc[rows] + y
            return carry
        lax.fori_loop(lo, hi, body, 0, unroll=2 if (hi - lo) % 2 == 0 else 1)

    groups = [[(step - nb, nb) for nb in range(lb) if 0 <= step - nb < la] for step in range(la + lb - 1)]
    early = max(1, len(groups) - 2)
    exchange1, exchange2 = [], []
    tail, todo = [], []
    for g, group in enumerate(groups):
        places = [(na, nb, nearest(p, la, na), nearest(q, lb, nb)) for na, nb in group]
        for na, nb, s, t in places:
            if g > 0:
                arrive(place(s, t, core))
            forward(na, nb, s, t)
        if g == 0:
            for copy in fetches:
                copy.start()
        todo += [(place(s, t, core), False) for _, _, s, t in places]
        if cores == 2:
            todo += [(place(s, t, 1 - core), True) for _, _, s, t in places]
        if g == 0 and early > 1:
            continue
        if g == min(1, early - 1):
            for copy in fetches:
                copy.wait()
        acc = acc1 if g < early else acc2
        last = g == len(groups) - 1
        for n, (block, remote) in enumerate(todo):
            if remote:
                arrive(block)
            first = g in (min(1, early - 1), early) and n == 0
            if last:
                multiply(block, acc, 1, n_col, first)
                tail.append((block, first))
            else:
                multiply(block, acc, 1, n_col + 1, first)
        todo = []
        if g == early - 1:
            for k in range(1, n_col):
                to = (col + k) % n_col
                copy = pltpu.make_async_remote_copy(
                    src_ref=acc1.at[pl.ds(to * bt, bt)], dst_ref=in1.at[k - 1], send_sem=s1.at[k - 1],
                    recv_sem=r1.at[k - 1], device_id={"col": to}, device_id_type=MESH)
                copy.start()
                exchange1.append(copy)
    for k in range(1, n_col):
        to = (col + k) % n_col
        out2[k - 1] = acc2[pl.ds(to * bt, bt)].astype(BF16)
        copy = pltpu.make_async_remote_copy(
            src_ref=out2.at[k - 1], dst_ref=in2.at[k - 1], send_sem=s2.at[k - 1],
            recv_sem=r2.at[k - 1], device_id={"col": to}, device_id_type=MESH)
        copy.start()
        exchange2.append(copy)
    for block, first in tail:
        multiply(block, acc2, n_col, n_col + 1, first)
    for copy in small:
        copy.wait()
    w = w_ref[...]
    classes, feats = w.shape
    lab = lab_ref[...]
    onehot = (lax.broadcasted_iota(jnp.int32, (classes, bt * tile), 0) == lab).astype(F32).astype(BF16)
    valid = jnp.where(lab >= 0, 1.0, 0.0).astype(F32)
    y = acc1[pl.ds(col * bt, bt)] + acc2[pl.ds(col * bt, bt)]
    for n, copy in enumerate(exchange1):
        copy.wait()
        y = y + in1[n]
    y = y.reshape(bt * tile, feats)
    hi, lo = split(y)
    picked = dot(onehot, hi) + dot(onehot, lo)
    for n, copy in enumerate(exchange2):
        copy.wait()
        late = in2[n].reshape(bt * tile, feats)
        picked = picked + dot(onehot, late)
        y = y + late.astype(F32)
    hi, lo = split(y)
    y_t = y.T
    hi_v, lo_v = split(y_t * valid)
    gram_hi, gram_lo = split(dot(hi_v, hi) + dot(hi_v, lo) + dot(lo_v, hi))
    total = dot(w, gram_hi) + dot(w, gram_lo) - picked

    per = lined.shape[1]
    owners = part.shape[0] // per
    part[pl.ds((owners - 1) * per, per)] = jnp.zeros((per, feats), F32)
    part[pl.ds(0, classes)] = total

    def rows(o):
        return pl.ds(pl.multiple_of(o * per, per), per)

    def owner(o):
        return True if owners == size else o < owners

    def term(k, to):
        return pltpu.make_async_remote_copy(
            src_ref=part.at[rows(to)], dst_ref=terms.at[k - 1], send_sem=s3.at[k - 1], recv_sem=r3.at[k - 1],
            device_id=device(p, (mine + k) % size), device_id_type=MESH)

    def across(k, source):
        return pltpu.make_async_remote_copy(
            src_ref=lined.at[source], dst_ref=lined.at[source], send_sem=s4.at[k - 1], recv_sem=r4.at[source],
            device_id=device((p + k) % la, mine), device_id_type=MESH)

    def result(k, o):
        return pltpu.make_async_remote_copy(
            src_ref=summed.at[rows(o)], dst_ref=summed.at[rows(o)], send_sem=s5.at[k - 1], recv_sem=r5.at[o],
            device_id=device(p, (mine + k) % size), device_id_type=MESH)

    def send_term(k):
        to = (mine + k) % size
        when(owner(to), lambda: term(k, to).start())
    loop(size, send_term)

    t_hi, t_lo = split(y_t)
    logits[...] = dot(w, t_hi) + dot(w, t_lo)

    def reduce():
        def add(k, value):
            term(k, 0).wait_recv()
            return value + terms[k - 1]
        lined[p] = lax.fori_loop(1, size, add, part[rows(mine)], unroll=size <= 8)
        loop(la, lambda k: across(k, p).start())
        loop(la, lambda k: across(k, (p + k) % la).wait_recv())
        value = lined[0]
        for n in range(1, la):
            value = value + lined[n]
        summed[rows(mine)] = value
        loop(size, lambda k: result(k, mine).start())
    when(owner(mine), reduce)

    def take(k):
        o = (mine + k) % size
        when(owner(o), lambda: result(k, o).wait_recv())
    loop(size, take)
    wgrad[...] = summed[pl.ds(0, classes)] * scale

    for cond, copy in started:
        when(cond, copy.wait_send)

    def sent(k):
        to = (mine + k) % size
        when(owner(to), lambda: term(k, to).wait_send())
        when(owner(mine), lambda: result(k, mine).wait_send())
    loop(size, sent)
    when(owner(mine), lambda: loop(la, lambda k: across(k, p).wait_send()))


def local(n_row, n_col, features, weight, labels, tile_rows, tile_cols, tile_count, tile_vals):
    la, lb, cores = factors(n_row)
    classes, tile, slots = weight.shape[1], tile_vals.shape[-1], tile_vals.shape[2]
    own, feat = features.shape
    bt = own // tile
    rt, ct = n_col * bt, n_row * bt
    nodes = own * n_row * n_col
    key = jnp.where(jnp.arange(slots, dtype=jnp.int32) < tile_count.reshape(()),
                    tile_rows.reshape(slots) * ct + tile_cols.reshape(slots), -1)
    match = key[:, None] == jnp.arange(rt * ct, dtype=jnp.int32)[None, :]
    table = slots + jnp.sum(jnp.where(match, jnp.arange(slots, dtype=jnp.int32)[:, None] - slots, 0), axis=0)
    dims = (n_row, n_col, la, lb, cores, 1.0 / math.sqrt(nodes))
    vmem = pl.BlockSpec(memory_space=pltpu.VMEM)
    anywhere = pl.BlockSpec(memory_space=pl.ANY)
    dma = pltpu.SemaphoreType.DMA
    peers = max(1, n_col - 1)
    size = lb * cores * n_col
    chunks = -(-classes // 8)
    per = 8 * -(-chunks // size)
    owners = -(-chunks * 8 // per)
    logits, wgrad = pl.pallas_call(
        functools.partial(kernel, dims),
        out_shape=(jax.ShapeDtypeStruct((classes, own), F32), jax.ShapeDtypeStruct((classes, feat), F32)),
        in_specs=[anywhere, anywhere, anywhere, pl.BlockSpec(memory_space=pltpu.SMEM), anywhere],
        out_specs=(vmem, vmem),
        scratch_shapes=[
            pltpu.VMEM((n_row, own, feat), BF16),
            pltpu.VMEM((slots + 1, tile, tile), BF16),
            pltpu.VMEM((rt, tile, feat), F32),
            pltpu.VMEM((rt, tile, feat), F32),
            pltpu.VMEM((peers, bt, tile, feat), BF16),
            pltpu.VMEM((peers, bt, tile, feat), F32),
            pltpu.VMEM((peers, bt, tile, feat), BF16),
            pltpu.VMEM((owners * per, feat), F32),
            pltpu.VMEM((size - 1, per, feat), F32),
            pltpu.VMEM((la, per, feat), F32),
            pltpu.VMEM((owners * per, feat), F32),
            pltpu.VMEM((classes, feat), BF16),
            pltpu.VMEM((1, own), jnp.int32),
            dma((la * lb, 5)), dma((n_row,)), dma((4,)), dma((3,)),
            dma((peers,)), dma((peers,)), dma((peers,)), dma((peers,)),
            dma((size - 1,)), dma((size - 1,)), dma((la - 1,)), dma((la,)), dma((size - 1,)), dma((owners,)),
        ],
        compiler_params=pltpu.CompilerParams(collective_id=0, has_side_effects=True, vmem_limit_bytes=60 * 2**20),
        cost_estimate=pl.CostEstimate(flops=2 * rt * ct * tile * tile * feat, bytes_accessed=slots * tile * tile * 2, transcendentals=0),
        name="aggregate",
    )(features, weight.T, labels.reshape(1, own), table, tile_vals.reshape(slots, tile, tile))
    return logits.T, wgrad.T


def solution(mesh):
    placed = (
        P(("col", "row"), None),
        P(),
        P(("row", "col")),
        P("row", "col", None),
        P("row", "col", None),
        P("row", "col"),
        P("row", "col", None, None, None),
    )
    body = functools.partial(local, mesh.shape["row"], mesh.shape["col"])
    return jax.shard_map(
        body, mesh=mesh, in_specs=placed, out_specs=(P(("row", "col"), None), P()), check_vma=False
    )
```
